256 devices in a mesh: grid: 64 (over y, z, core), layer: 4 (over x).
Axes of the slice: x: 4, y: 4, z: 8, core: 2. Of those that a mesh axis runs over, the one named last changes fastest.
Arguments:
- h_vals: bfloat16 [256, 28, 128, 128], P('grid', 'layer'), may hold values from -0.09375 to 0.09375
- h_cols: int32 [256, 28], P('grid', 'layer'), may hold values from 0 to 255, as said below
- t_now: bfloat16 [256, 28, 128, 128], P(('grid', 'layer')), may hold values from -6 to 6
- t_prev: bfloat16 [256, 28, 128, 128], P(('grid', 'layer')), may hold values from -6 to 6
- t_cols: int32 [256, 28], replicated, may hold values from 0 to 255, as said below
- density: float32 [256, 28, 128, 128], P(('grid', 'layer')), may hold values from -6 to 6
- coefficient: float32 [1], replicated, may hold values from 0.5 to 1.5
Outputs:
- t_next: bfloat16 [256, 28, 128, 128], P(('grid', 'layer'))
- density_next: float32 [256, 28, 128, 128], P(('grid', 'layer'))
The draws below stay inside these ranges and needn't reach their ends.
Inputs may be any that keep to these rules, and one draw needn't show every extreme that they name: Each row of h_cols holds distinct block columns within 15 of the row's own index, taken cyclically modulo 256; slots 7 l to 7 l + 6 hold columns c with c % 4 == l. Each row of t_cols holds distinct block columns within 15 of the row's own index, taken cyclically modulo 256.
All inputs are finite; a program needn't handle non-finite values.
Results may differ from the reference program's by a relative error of at most 0.0065.
Values may be sent and summed in bfloat16 or wider, within the bound.
No kernel may reach another device: no remote copies, remote signals or barrier semaphores. Data moves between devices by JAX's collectives and lax.ppermute only.
A program may use at most 128 MiB of HBM per device.

```python
import jax
import jax.numpy as jnp
from jax import lax

B = 128
K = 28
HW = 15
TR = 1
NB = 256
N_LAYER = 4


def band_table():
    width = 2 * HW + 1
    rows = jnp.arange(NB, dtype=jnp.int32)
    offsets = jnp.arange(width, dtype=jnp.int32)
    return ((rows[:, None] - HW + offsets[None, :]) % NB, offsets)


def draw_h_cols(key, part):
    key = jax.random.fold_in(key, 11)
    candidates, offsets = band_table()
    scores = jax.random.randint(key, candidates.shape, 0, 1 << 20, dtype=jnp.int32) * 64 + offsets[None, :]
    per_layer = K // N_LAYER
    pieces = []
    for layer_id in range(N_LAYER):
        allowed = candidates // TR % N_LAYER == layer_id
        masked = jnp.where(allowed, scores, -1)
        best, where = lax.top_k(masked, per_layer)
        pieces.append(jnp.take_along_axis(candidates, where, axis=1))
    return jnp.concatenate(pieces, axis=1).astype(jnp.int32)


def draw_t_cols(key, part):
    key = jax.random.fold_in(key, 12)
    candidates, offsets = band_table()
    scores = jax.random.randint(key, candidates.shape, 0, 1 << 20, dtype=jnp.int32) * 64 + offsets[None, :]
    best, where = lax.top_k(scores, K)
    return jnp.take_along_axis(candidates, where, axis=1).astype(jnp.int32)


def block_scale(key, shape, shards, least, high):
    level = 1.0
    for position, parts in shards:
        draws = jax.random.uniform(jax.random.fold_in(jax.random.fold_in(key, 6), position), (parts,), jnp.float32, least / len(shards), high / len(shards))
        level = level * jnp.repeat(jnp.exp(draws), shape[position] // parts).reshape((-1,) + (1,) * (len(shape) - 1 - position))
    return level


def gaussian(own_key, shape, scale, reach, shards=(), kind=jnp.bfloat16):
    entries = scale * jax.random.normal(own_key, shape, jnp.float32)
    if shards:
        entries = entries * block_scale(own_key, shape, shards, -0.22, 0.18)
    return jnp.clip(entries, -reach, reach).astype(kind)


def setup_inputs(seed: int = 0) -> dict:
    keys = jax.random.split(jax.random.key(seed), 8)
    h_vals = gaussian(keys[0], (NB, K, B, B), (K * B) ** -0.5, 0.09375, ((0, 64), (1, 4)))
    h_cols = draw_h_cols(jax.random.fold_in(keys[7], 71), 0)
    t_now = gaussian(keys[2], (NB, K, B, B), 1.0, 6.0, ((0, 256),))
    t_prev = gaussian(keys[3], (NB, K, B, B), 1.0, 6.0, ((0, 256),))
    t_cols = draw_t_cols(jax.random.fold_in(keys[7], 71), 0)
    density = gaussian(keys[5], (NB, K, B, B), 1.0, 6.0, ((0, 256),), jnp.float32)
    coefficient = jnp.clip(jax.random.uniform(keys[6], (1,), jnp.float32, 0.5, 1.5), 0.5, 1.5)
    return {"h_vals": h_vals, "h_cols": h_cols, "t_now": t_now, "t_prev": t_prev, "t_cols": t_cols, "density": density, "coefficient": coefficient}


def reference(h_vals, h_cols, t_now, t_prev, t_cols, density, coefficient):
    slots = jnp.arange(K, dtype=jnp.int32)
    flat = t_now.reshape(NB * K, B, B)

    def one_row(row):
        cols = h_cols[row]
        wanted = t_cols[row]
        present = t_cols[cols]
        equal = wanted[None, :, None] == present[:, None, :]
        pick = jnp.sum(jnp.where(equal, slots[None, None, :], 0), axis=2).astype(jnp.int32)
        valid = jnp.any(equal, axis=2)
        index = (cols[:, None] * K + pick).astype(jnp.int32)
        chosen = jnp.where(valid[:, :, None, None], flat[index], jnp.zeros((), flat.dtype))
        return jnp.einsum("hab,hsbc->sac", h_vals[row].astype(jnp.float32), chosen.astype(jnp.float32))

    product = lax.map(one_row, jnp.arange(NB, dtype=jnp.int32))
    t_next = (2.0 * product - t_prev.astype(jnp.float32)).astype(jnp.bfloat16)
    density_next = density + coefficient[0] * t_next.astype(jnp.float32)
    return t_next, density_next
```

```python
import functools

import jax
import jax.numpy as jnp
import numpy as np
from jax import lax
from jax.experimental import pallas as pl
from jax.experimental.pallas import tpu as pltpu
from jax.sharding import PartitionSpec as P

HW = 15
B = 128
K = 28
NB = 256
N_LAYER = 4
GROUP = 8
WIN = 4
EXTRA = 16
ROWS = WIN * B + EXTRA
NEAR = 24
FAR = 7
WIDE = 5
VMEM = 50 * 2**20


def halo_lists(step):
    far, near = [], []
    for cls in range(GROUP):
        got = {1: [], 2: []}
        for row in range(GROUP):
            for slot in range(WIN):
                col = cls + GROUP * (slot - 2 + (row > cls))
                if abs(col - row) > HW:
                    continue
                for dist in (1, 2):
                    at = GROUP * dist * step
                    if any(abs(out + at - row) <= HW and abs(out + at - col) <= HW for out in range(GROUP)):
                        got[dist].append(row * WIN + slot)
        assert set(got[2]) <= set(got[1])
        far.append(got[2])
        near.append([x for x in got[1] if x not in got[2]])
    return far, near


def table():
    lists = [*halo_lists(1), *halo_lists(-1)]
    sizes = [max(len(x) for x in part) for part in lists]
    rows = [sum(([*part[cls], *([-1] * (size - len(part[cls])))] for part, size in zip(lists, sizes)), []) for cls in range(GROUP)]
    return np.array(rows, np.int32), sizes


TABLE, SIZES = table()
STARTS = [sum(SIZES[:i]) for i in range(4)]


def whole(space=pltpu.VMEM):
    return pl.BlockSpec(memory_space=space)


def params():
    return pltpu.CompilerParams(vmem_limit_bytes=VMEM)


def window_place(col, own_row):
    ahead = (col - own_row + NB // 2) % NB - NB // 2 + 16
    return (own_row + ahead) % GROUP * WIN + ahead // GROUP


def spread_kernel(where_ref, t_ref, cols_ref, h_cols_ref, out_ref, cols, tile, sem):
    row = where_ref[0]
    base = pl.multiple_of(row // GROUP * GROUP, GROUP)
    copy = pltpu.make_async_copy(cols_ref.at[pl.ds(base, GROUP)], cols, sem)
    copy.start()
    tile[...] = jnp.zeros_like(tile)
    tile[0 : h_cols_ref.shape[0], 0 : h_cols_ref.shape[1]] = h_cols_ref[...].astype(jnp.float32)
    extra = tile[...].astype(jnp.bfloat16)
    for cls in range(GROUP):
        out_ref[cls, 0 : WIN * B, :] = jnp.zeros((WIN * B, B), jnp.bfloat16)
        out_ref[cls, WIN * B : ROWS, :] = extra
    copy.wait()
    for slot in range(K):
        place = window_place(cols[row % GROUP, slot], row)
        start = pl.multiple_of(place % WIN * B, B)
        out_ref[place // WIN, pl.ds(start, B), :] = t_ref[0, slot]


def spread(where, t_now, t_cols, h_cols):
    return pl.pallas_call(
        spread_kernel,
        out_shape=jax.ShapeDtypeStruct((GROUP, ROWS, B), jnp.bfloat16),
        in_specs=[whole(pltpu.SMEM), whole(), whole(pl.ANY), whole()],
        out_specs=whole(),
        scratch_shapes=[pltpu.SMEM((GROUP, K), jnp.int32), pltpu.VMEM((EXTRA, B), jnp.float32), pltpu.SemaphoreType.DMA],
        compiler_params=params(),
        name="spread",
    )(where, t_now, t_cols, h_cols)


def pack_kernel(where_ref, tab_ref, x_ref, *out_refs):
    cls = where_ref[1]
    for out_ref, first, size in zip(out_refs, STARTS, SIZES):
        for at in range(size):
            entry = jnp.maximum(tab_ref[cls, first + at], 0)
            start = pl.multiple_of(entry % WIN * B, B)
            out_ref[at] = x_ref[entry // WIN, pl.ds(start, B), :]


def pack(where, tab, x):
    return pl.pallas_call(
        pack_kernel,
        out_shape=[jax.ShapeDtypeStruct((size, B, B), jnp.bfloat16) for size in SIZES],
        in_specs=[whole(pltpu.SMEM), whole(pltpu.SMEM), whole()],
        out_specs=[whole()] * 4,
        compiler_params=params(),
        name="pack",
    )(where, tab, x)


def near_kernel(where_ref, tab_ref, hc_ref, x_ref, rf_ref, rn_ref, lf_ref, ln_ref, h_ref, acc_ref, far_ref, hd, xd):
    cls = where_ref[1]
    hd[...] = jnp.zeros_like(hd)
    far_ref[...] = jnp.zeros_like(far_ref)
    xd[...] = jnp.zeros_like(xd)

    @pl.loop(0, GROUP)
    def _(source):
        for r in range(N_LAYER):
            out_row = source // N_LAYER * N_LAYER + r
            start = pl.multiple_of(out_row * B, B)
            for slot in range(K // N_LAYER):
                at = hc_ref[source, r * (K // N_LAYER) + slot]
                block = h_ref[source, r, slot]
                is_near = jnp.logical_and(at >= GROUP, at < GROUP + NEAR)

                @pl.when(is_near)
                def _():
                    hd[at - GROUP, pl.ds(start, B), :] = block

                @pl.when(jnp.logical_not(is_near))
                def _():
                    far_ref[jnp.where(at < GROUP, at - 1, at - (GROUP + NEAR) + FAR), pl.ds(start, B), :] = block

    for row in range(GROUP):
        for slot in range(WIN):
            xd[slot + (row > cls).astype(jnp.int32), (GROUP + row) * B : (GROUP + row + 1) * B, :] = x_ref[row, slot * B : (slot + 1) * B, :]
    for ref, first, size, dist in zip((rf_ref, rn_ref, lf_ref, ln_ref), STARTS, SIZES, (-1, -1, 1, 1)):
        for at in range(size):
            entry = tab_ref[cls, first + at]
            row, slot = entry // WIN, entry % WIN
            col = slot + (row > cls).astype(jnp.int32) + dist
            start = jnp.where(entry >= 0, (GROUP * (1 + dist) + row) * B, NEAR * B)
            xd[jnp.clip(col, 0, WIDE - 1), pl.ds(pl.multiple_of(start, B), B), :] = ref[at]

    @pl.loop(0, 2)
    def _(half):
        rows = pl.ds(pl.multiple_of(half * (4 * B), 4 * B), 4 * B)
        left = jnp.concatenate([hd[n, rows, :] for n in range(NEAR)], axis=1)
        for col in range(0, WIDE, 2):
            wide = min(2, WIDE - col)
            right = jnp.concatenate([xd[col + i, 0 : NEAR * B, :] for i in range(wide)], axis=1)
            got = jnp.dot(left, right, preferred_element_type=jnp.float32)
            for i in range(wide):
                acc_ref[col + i, rows, :] = got[:, i * B : (i + 1) * B]


def near(where, tab, hc, x, rf, rn, lf, ln, h):
    return pl.pallas_call(
        near_kernel,
        out_shape=[
            jax.ShapeDtypeStruct((WIDE, GROUP * B, B), jnp.float32),
            jax.ShapeDtypeStruct((2 * FAR, GROUP * B, B), jnp.bfloat16),
        ],
        in_specs=[whole(pltpu.SMEM)] * 3 + [whole()] * 6,
        out_specs=[whole()] * 2,
        scratch_shapes=[pltpu.VMEM((NEAR, GROUP * B, B), jnp.bfloat16), pltpu.VMEM((WIDE, (NEAR + 1) * B, B), jnp.bfloat16)],
        compiler_params=params(),
        cost_estimate=pl.CostEstimate(flops=2 * 1024 * 3072 * 640, bytes_accessed=20_000_000, transcendentals=0),
        name="near",
    )(where, tab, hc, x, rf, rn, lf, ln, h)


def far_kernel(where_ref, tab_ref, acc_ref, far_ref, r_ref, l_ref, out_ref, xd, sums):
    cls = where_ref[1]
    xd[...] = jnp.zeros_like(xd)
    for side, (ref, first, size) in enumerate(((r_ref, STARTS[0], SIZES[0]), (l_ref, STARTS[2], SIZES[2]))):
        for at in range(size):
            entry = tab_ref[cls, first + at]
            row, slot = entry // WIN, entry % WIN
            col = slot + (row > cls).astype(jnp.int32) - (0 if side else 2)
            start = jnp.where(entry >= 0, (row if side else row - 1) * B, FAR * B)
            xd[side, jnp.clip(col, 0, 2), pl.ds(pl.multiple_of(start, B), B), :] = ref[at]

    @pl.loop(0, 2)
    def _(half):
        rows = pl.ds(pl.multiple_of(half * (4 * B), 4 * B), 4 * B)
        got = []
        for side in range(2):
            left = jnp.concatenate([far_ref[side * FAR + n, rows, :] for n in range(FAR)], axis=1)
            right = jnp.concatenate([xd[side, i, 0 : FAR * B, :] for i in range(3)], axis=1)
            got.append(jnp.dot(left, right, preferred_element_type=jnp.float32))
        for col in range(WIDE):
            total = acc_ref[col, rows, :]
            if col <= 2:
                total = total + got[0][:, col * B : (col + 1) * B]
            if col >= 2:
                total = total + got[1][:, (col - 2) * B : (col - 1) * B]
            sums[col, rows, :] = total.astype(jnp.bfloat16)

    for row in range(GROUP):
        for slot in range(WIN):
            out_ref[row, slot] = sums[slot + (row > cls).astype(jnp.int32), row * B : (row + 1) * B, :]


def far(where, tab, acc, far_h, fr, fl):
    return pl.pallas_call(
        far_kernel,
        out_shape=jax.ShapeDtypeStruct((GROUP, WIN, B, B), jnp.bfloat16),
        in_specs=[whole(pltpu.SMEM)] * 2 + [whole()] * 4,
        out_specs=whole(),
        scratch_shapes=[pltpu.VMEM((2, 3, (FAR + 1) * B, B), jnp.bfloat16), pltpu.VMEM((WIDE, GROUP * B, B), jnp.bfloat16)],
        compiler_params=params(),
        cost_estimate=pl.CostEstimate(flops=4 * 1024 * 896 * 384, bytes_accessed=8_000_000, transcendentals=0),
        name="far",
    )(where, tab, acc, far_h, fr, fl)


def update_kernel(where_ref, coef_ref, got_ref, cols_ref, prev_ref, density_ref, next_ref, out_ref, cols, sem):
    row = where_ref[0]
    step = pl.program_id(0)

    @pl.when(step == 0)
    def _():
        base = pl.multiple_of(row // GROUP * GROUP, GROUP)
        copy = pltpu.make_async_copy(cols_ref.at[pl.ds(base, GROUP)], cols, sem)
        copy.start()
        copy.wait()

    for i in range(4):
        place = window_place(cols[row % GROUP, step * 4 + i], row)
        product = got_ref[place // WIN, place % WIN].astype(jnp.float32)
        fresh = (2.0 * product - prev_ref[0, i].astype(jnp.float32)).astype(jnp.bfloat16)
        next_ref[0, i] = fresh
        out_ref[0, i] = density_ref[0, i] + coef_ref[0] * fresh.astype(jnp.float32)


def update(where, coefficient, got, t_cols, t_prev, density):
    blocks = pl.BlockSpec((1, 4, B, B), lambda i: (0, i, 0, 0))
    return pl.pallas_call(
        update_kernel,
        grid=(K // 4,),
        out_shape=[jax.ShapeDtypeStruct((1, K, B, B), jnp.bfloat16), jax.ShapeDtypeStruct((1, K, B, B), jnp.float32)],
        in_specs=[whole(pltpu.SMEM), whole(pltpu.SMEM), whole(), whole(pl.ANY), blocks, blocks],
        out_specs=[blocks, blocks],
        scratch_shapes=[pltpu.SMEM((GROUP, K), jnp.int32), pltpu.SemaphoreType.DMA],
        compiler_params=params(),
        name="update",
    )(where, coefficient, got, t_cols, t_prev, density)


def shards(h_vals, h_cols, t_now, t_prev, t_cols, density, coefficient):
    chips = lax.axis_size("grid") // 2
    groups = [[(2 * q + core) * N_LAYER + x for core in range(2) for x in range(N_LAYER)] for q in range(chips)]
    axes = ("grid", "layer")
    exchange = functools.partial(lax.all_to_all, axis_name=axes, split_axis=0, concat_axis=0, axis_index_groups=groups, tiled=True)

    def shift(block, step):
        count = lax.axis_size("grid")
        return lax.ppermute(block, "grid", [(i, (i + 2 * step) % count) for i in range(count)])

    grid_pos = lax.axis_index("grid")
    layer_pos = lax.axis_index("layer")
    own_row = grid_pos * N_LAYER + layer_pos
    where = jnp.stack([own_row, own_row % GROUP]).astype(jnp.int32)
    tab = jnp.asarray(TABLE)

    h_all = lax.all_gather(h_vals, axes, axis=0, axis_index_groups=groups)
    x = exchange(spread(where, t_now, t_cols, h_cols))
    hc = x[:, WIN * B : WIN * B + N_LAYER, 0 : K // N_LAYER].astype(jnp.int32)
    hc = ((hc - own_row // GROUP * GROUP + 2 * GROUP) % NB).reshape(GROUP, K)
    right_far, right_near, left_far, left_near = pack(where, tab, x)
    rf, lf = shift(right_far, 1), shift(left_far, -1)
    rn, ln = shift(right_near, 1), shift(left_near, -1)
    rff, lff = shift(rf, 1), shift(lf, -1)
    acc, far_h = near(where, tab, hc, x, rf, rn, lf, ln, h_all)
    sums = far(where, tab, acc, far_h, rff, lff)
    got = exchange(sums)
    return tuple(update(where, coefficient, got, t_cols, t_prev, density))


def solution(mesh):
    rows = P(("grid", "layer"), None, None, None)
    placed = (P("grid", "layer", None, None), P("grid", "layer"), rows, rows, P(), rows, P())
    return jax.shard_map(shards, mesh=mesh, in_specs=placed, out_specs=(rows, rows), check_vma=False)
```

```python
import functools

import jax
import jax.numpy as jnp
import numpy as np
from jax import lax
from jax.experimental import pallas as pl
from jax.experimental.pallas import tpu as pltpu
from jax.sharding import PartitionSpec as P

HW = 15
B = 128
K = 28
NB = 256
N_LAYER = 4
GROUP = 8
WIN = 4
EXTRA = 16
ROWS = WIN * B + EXTRA
NEAR = 24
FAR = 7
WIDE = 5
MIB = 2**20


def halo_lists(step):
    far, near = [], []
    for cls in range(GROUP):
        got = {1: [], 2: []}
        for row in range(GROUP):
            for slot in range(WIN):
                col = cls + GROUP * (slot - 2 + (row > cls))
                if abs(col - row) > HW:
                    continue
                for dist in (1, 2):
                    at = GROUP * dist * step
                    if any(abs(out + at - row) <= HW and abs(out + at - col) <= HW for out in range(GROUP)):
                        got[dist].append(row * WIN + slot)
        assert set(got[2]) <= set(got[1])
        far.append(got[2])
        near.append([x for x in got[1] if x not in got[2]])
    return far, near


def table():
    lists = [*halo_lists(1), *halo_lists(-1)]
    sizes = [max(len(x) for x in part) for part in lists]
    rows = [sum(([*part[cls], *([-1] * (size - len(part[cls])))] for part, size in zip(lists, sizes)), []) for cls in range(GROUP)]
    return np.array(rows, np.int32), sizes


TABLE, SIZES = table()
STARTS = [sum(SIZES[:i]) for i in range(4)]


def whole(space=pltpu.VMEM):
    return pl.BlockSpec(memory_space=space)


def in_hbm(x):
    return pltpu.with_memory_space_constraint(x, pltpu.HBM)


def params(mib):
    return pltpu.CompilerParams(vmem_limit_bytes=mib * MIB)


def absent(present_at, size):
    every = jnp.arange(size, dtype=jnp.int32)
    missing = jnp.all(present_at[..., None, :] != every[:, None], axis=-1)
    rank = jnp.sum(jnp.where(every[None, :] < every[:, None], missing[..., None, :], False).astype(jnp.int32), axis=-1)
    wanted = jnp.arange(size - present_at.shape[-1], dtype=jnp.int32)
    hit = jnp.logical_and(missing[..., None, :], rank[..., None, :] == wanted[:, None])
    return jnp.sum(jnp.where(hit, every, 0), axis=-1)


def spread_kernel(where_ref, t_ref, cols_ref, h_cols_ref, out_ref, places_ref, cols, tile, cols_sem, sem):
    row = where_ref[0]
    half = pl.multiple_of(row // B * B, B)
    load = pltpu.make_async_copy(cols_ref.at[:, pl.ds(half, B)], cols, cols_sem)
    load.start()
    tile[...] = jnp.zeros_like(tile)
    tile[0 : h_cols_ref.shape[0], 0 : h_cols_ref.shape[1]] = h_cols_ref[...].astype(jnp.float32)
    for cls in range(GROUP):
        out_ref[cls, 0 : WIN * B, :] = jnp.zeros((WIN * B, B), jnp.bfloat16)
        out_ref[cls, WIN * B : ROWS, :] = tile[...].astype(jnp.bfloat16)
    load.wait()
    for slot in range(K):
        ahead = (cols[slot, row % B] - row + NB // 2) % NB - NB // 2 + 2 * GROUP
        place = (row + ahead) % GROUP * WIN + ahead // GROUP
        places_ref[slot] = place
        start = pl.multiple_of(place % WIN * B, B)
        pltpu.make_async_copy(t_ref.at[0, slot], out_ref.at[place // WIN, pl.ds(start, B)], sem).start()
    pltpu.make_async_copy(t_ref, t_ref, sem).wait()


def spread(where, t_now, t_cols, h_cols):
    return pl.pallas_call(
        spread_kernel,
        out_shape=[jax.ShapeDtypeStruct((GROUP, ROWS, B), jnp.bfloat16), jax.ShapeDtypeStruct((K,), jnp.int32)],
        in_specs=[whole(pltpu.SMEM), whole(pltpu.HBM), whole(pltpu.HBM), whole()],
        out_specs=[whole(), whole(pltpu.SMEM)],
        scratch_shapes=[
            pltpu.SMEM((K, B), jnp.int32),
            pltpu.VMEM((EXTRA, B), jnp.float32),
            pltpu.SemaphoreType.DMA,
            pltpu.SemaphoreType.DMA,
        ],
        compiler_params=params(8),
        name="spread",
    )(where, in_hbm(t_now), in_hbm(t_cols.T), h_cols)


def pack_kernel(parts, where_ref, tab_ref, x_ref, *refs):
    out_refs = refs[(len(refs) - len(parts)) // 2 :][: len(parts)]
    cls = where_ref[1]
    for out_ref, part in zip(out_refs, parts):
        for at in range(SIZES[part]):
            entry = jnp.maximum(tab_ref[cls, STARTS[part] + at], 0)
            start = pl.multiple_of(entry % WIN * B, B)
            out_ref[at] = x_ref[entry // WIN, pl.ds(start, B), :]


def pack(where, tab, x, parts, held):
    return pl.pallas_call(
        functools.partial(pack_kernel, parts),
        out_shape=[jax.ShapeDtypeStruct((SIZES[part], B, B), jnp.bfloat16) for part in parts]
        + [jax.ShapeDtypeStruct(h.shape, h.dtype) for h in held],
        in_specs=[whole(pltpu.SMEM), whole(pltpu.SMEM), whole()] + [whole(pltpu.HBM)] * len(held),
        out_specs=[whole()] * len(parts) + [whole(pltpu.HBM)] * len(held),
        input_output_aliases={3 + i: len(parts) + i for i in range(len(held))},
        compiler_params=params(8),
        name="pack",
    )(where, tab, x, *map(in_hbm, held))


def merge_kernel(first_ref, second_ref, out_ref, sems):
    half = first_ref.shape[0]
    copies = [pltpu.make_async_copy(ref, out_ref.at[i * half : (i + 1) * half], sems.at[i]) for i, ref in enumerate((first_ref, second_ref))]
    for copy in copies:
        copy.start()
    for copy in copies:
        copy.wait()


def merge(first, second):
    return pl.pallas_call(
        merge_kernel,
        out_shape=jax.ShapeDtypeStruct((2 * first.shape[0], *first.shape[1:]), first.dtype),
        in_specs=[whole(pltpu.HBM)] * 2,
        out_specs=whole(pltpu.HBM),
        scratch_shapes=[pltpu.SemaphoreType.DMA((2,))],
        compiler_params=params(4),
        name="merge",
    )(in_hbm(first), in_hbm(second))


def after_kernel(*_):
    pass


def after(held, *first):
    return pl.pallas_call(
        after_kernel,
        out_shape=jax.ShapeDtypeStruct(held.shape, held.dtype),
        in_specs=[whole(pltpu.HBM)] + [whole(pl.ANY)] * len(first),
        out_specs=whole(pltpu.HBM),
        input_output_aliases={0: 0},
        compiler_params=params(4),
        name="after",
    )(in_hbm(held), *first)


H_PARTS = (((0, 0),), ((0, 1),), ((-1, 0),), ((1, 1),), ((-1, 1), (2, 0)), ((1, 0), (2, 1)))


def near_kernel(where_ref, tab_ref, h_at_ref, x_ref, rf_ref, rn_ref, lf_ref, ln_ref, *refs):
    *h_refs, acc_ref, far_ref, hd, xd, sem = refs
    cls = where_ref[1]

    own_core = cls // N_LAYER
    for h_ref, parts in zip(h_refs, H_PARTS):
        for number, (apart, other) in enumerate(parts):
            core = 1 - own_core if other else own_core
            layer = (cls + apart * (1 - 2 * own_core) + N_LAYER) % N_LAYER

            @pl.loop(0, N_LAYER)
            def _(r):
                out_row = core * N_LAYER + r
                rows = pl.ds(pl.multiple_of(out_row * B, B), B)
                for slot in range(K // N_LAYER):
                    at = h_at_ref[out_row, layer * (K // N_LAYER) + slot]
                    pltpu.make_async_copy(h_ref.at[number * N_LAYER + r, slot], hd.at[at, rows], sem).start()

    @pl.loop(0, GROUP)
    def _(out_row):
        rows = pl.ds(pl.multiple_of(out_row * B, B), B)
        for i in range(K, NEAR + GROUP):
            hd[h_at_ref[out_row, i], rows, :] = jnp.zeros((B, B), jnp.bfloat16)

    xd[...] = jnp.zeros_like(xd)
    for row in range(GROUP):
        for slot in range(WIN):
            xd[slot + (row > cls).astype(jnp.int32), (GROUP + row) * B : (GROUP + row + 1) * B, :] = x_ref[row, slot * B : (slot + 1) * B, :]
    for ref, first, size, dist in zip((rf_ref, rn_ref, lf_ref, ln_ref), STARTS, SIZES, (-1, -1, 1, 1)):
        for i in range(size):
            entry = tab_ref[cls, first + i]
            row, slot = entry // WIN, entry % WIN
            col = slot + (row > cls).astype(jnp.int32) + dist
            start = jnp.where(entry >= 0, (GROUP * (1 + dist) + row) * B, NEAR * B)
            xd[jnp.clip(col, 0, WIDE - 1), pl.ds(pl.multiple_of(start, B), B), :] = ref[i]
    pltpu.make_async_copy(hd.at[0:K], hd.at[0:K], sem).wait()

    @pl.loop(0, GROUP)
    def _(out_row):
        rows = pl.ds(pl.multiple_of(out_row * B, B), B)
        for i in range(GROUP):
            far_ref[i, rows, :] = hd[NEAR + i, rows, :]
        shift = (out_row > cls).astype(jnp.int32)
        left = jnp.concatenate([hd[n, rows, :] for n in range(NEAR)], axis=1)
        for slot in range(0, WIN, 2):
            right = jnp.concatenate([xd[slot + i + shift, 0 : NEAR * B, :] for i in range(2)], axis=1)
            got = jnp.dot(left, right, preferred_element_type=jnp.float32)
            for i in range(2):
                acc_ref[out_row, slot + i] = got[:, i * B : (i + 1) * B]


def near(where, tab, h_at, x, rf, rn, lf, ln, h_parts):
    return pl.pallas_call(
        near_kernel,
        out_shape=[
            jax.ShapeDtypeStruct((GROUP, WIN, B, B), jnp.float32),
            jax.ShapeDtypeStruct((GROUP, GROUP * B, B), jnp.bfloat16),
        ],
        in_specs=[whole(pltpu.SMEM)] * 3 + [whole()] * 5 + [whole(pltpu.HBM)] * len(h_parts),
        out_specs=[whole()] * 2,
        scratch_shapes=[
            pltpu.VMEM((NEAR + GROUP, GROUP * B, B), jnp.bfloat16),
            pltpu.VMEM((WIDE, (NEAR + 1) * B, B), jnp.bfloat16),
            pltpu.SemaphoreType.DMA,
        ],
        compiler_params=params(30),
        cost_estimate=pl.CostEstimate(flops=2 * 1024 * 3072 * 512, bytes_accessed=20_000_000, transcendentals=0),
        name="near",
    )(where, tab, h_at, x, rf, rn, lf, ln, *map(in_hbm, h_parts))


def far_kernel(where_ref, tab_ref, acc_ref, far_ref, r_ref, l_ref, out_ref, xd):
    cls = where_ref[1]
    xd[...] = jnp.zeros_like(xd)
    for ref, first, size, dist in ((r_ref, STARTS[0], SIZES[0], -2), (l_ref, STARTS[2], SIZES[2], 2)):
        for i in range(size):
            entry = tab_ref[cls, first + i]
            row, slot = entry // WIN, entry % WIN
            col = slot + (row > cls).astype(jnp.int32) + dist
            start = jnp.where(entry >= 0, (GROUP * (dist // 2 + 1) // 2 + row) * B, 2 * GROUP * B)
            xd[jnp.clip(col, 0, WIDE - 1), pl.ds(pl.multiple_of(start, B), B), :] = ref[i]

    @pl.loop(0, GROUP)
    def _(out_row):
        first = pl.multiple_of(out_row * B, B)
        shift = (out_row > cls).astype(jnp.int32)
        left = jnp.concatenate([far_ref[n, pl.ds(first, B), :] for n in range(GROUP)], axis=1)
        for slot in range(0, WIN, 2):
            right = jnp.concatenate([xd[slot + i + shift, pl.ds(first, GROUP * B), :] for i in range(2)], axis=1)
            got = jnp.dot(left, right, preferred_element_type=jnp.float32)
            for i in range(2):
                out_ref[out_row, slot + i] = (acc_ref[out_row, slot + i] + got[:, i * B : (i + 1) * B]).astype(jnp.bfloat16)


def far(where, tab, acc, far_h, fr, fl):
    return pl.pallas_call(
        far_kernel,
        out_shape=jax.ShapeDtypeStruct((GROUP, WIN, B, B), jnp.bfloat16),
        in_specs=[whole(pltpu.SMEM)] * 2 + [whole()] * 4,
        out_specs=whole(),
        scratch_shapes=[pltpu.VMEM((WIDE, (2 * GROUP + 1) * B, B), jnp.bfloat16)],
        compiler_params=params(16),
        cost_estimate=pl.CostEstimate(flops=2 * 1024 * 1024 * 512, bytes_accessed=8_000_000, transcendentals=0),
        name="far",
    )(where, tab, acc, far_h, fr, fl)


CHUNK = 4


def update_kernel(places_ref, coef_ref, got_ref, density_ref, prev_hbm, next_hbm, out_hbm, prev, fresh, out, prev_sem, next_sem, out_sem):
    def at(ref, part):
        return ref.at[0, part * CHUNK : (part + 1) * CHUNK]

    def copies(part):
        return (
            pltpu.make_async_copy(at(prev_hbm, part), at(prev, part), prev_sem.at[part]),
            pltpu.make_async_copy(at(fresh, part), at(next_hbm, part), next_sem.at[part]),
            pltpu.make_async_copy(at(out, part), at(out_hbm, part), out_sem.at[part]),
        )

    for part in range(K // CHUNK):
        copies(part)[0].start()
    for part in range(K // CHUNK):
        load, *stores = copies(part)
        load.wait()
        for slot in range(part * CHUNK, (part + 1) * CHUNK):
            place = places_ref[slot]
            product = got_ref[place // WIN, place % WIN].astype(jnp.float32)
            value = (2.0 * product - prev[0, slot].astype(jnp.float32)).astype(jnp.bfloat16)
            fresh[0, slot] = value
            out[0, slot] = density_ref[0, slot] + coef_ref[0] * value.astype(jnp.float32)
        for store in stores:
            store.start()
    for part in range(K // CHUNK):
        copies(part)[1].wait()
        copies(part)[2].wait()


def update(places, coefficient, got, density, t_prev):
    shape = (1, K, B, B)
    sems = pltpu.SemaphoreType.DMA((K // CHUNK,))
    return pl.pallas_call(
        update_kernel,
        out_shape=[jax.ShapeDtypeStruct(shape, jnp.bfloat16), jax.ShapeDtypeStruct(shape, jnp.float32)],
        in_specs=[whole(pltpu.SMEM), whole(pltpu.SMEM), whole(), whole(), whole(pltpu.HBM)],
        out_specs=[whole(pltpu.HBM)] * 2,
        scratch_shapes=[pltpu.VMEM(shape, jnp.bfloat16), pltpu.VMEM(shape, jnp.bfloat16), pltpu.VMEM(shape, jnp.float32), sems, sems, sems],
        compiler_params=params(16),
        name="update",
    )(places, coefficient, got, density, in_hbm(t_prev))


def shards(h_vals, h_cols, t_now, t_prev, t_cols, density, coefficient):
    chips = lax.axis_size("grid") // 2
    groups = [[(2 * q + core) * N_LAYER + x for core in range(2) for x in range(N_LAYER)] for q in range(chips)]
    axes = ("grid", "layer")
    exchange = functools.partial(lax.all_to_all, axis_name=axes, split_axis=0, concat_axis=0, axis_index_groups=groups, tiled=True)

    def shift(block, step):
        count = lax.axis_size("grid")
        return lax.ppermute(block, "grid", [(i, (i + 2 * step) % count) for i in range(count)])

    def along(block):
        route = [(g * N_LAYER + x, g * N_LAYER + (x + 1 - 2 * (g % 2)) % N_LAYER) for g in range(2 * chips) for x in range(N_LAYER)]
        return lax.ppermute(block, axes, route)

    def across(block):
        return lax.ppermute(block, "grid", [(i, i ^ 1) for i in range(2 * chips)])

    own_row = lax.axis_index("grid") * N_LAYER + lax.axis_index("layer")
    where = jnp.stack([own_row, own_row % GROUP]).astype(jnp.int32)
    tab = jnp.asarray(TABLE)

    h_one, h_other = along(h_vals), across(h_vals)
    spread_t, places = spread(where, t_now, t_cols, h_cols)
    x = exchange(spread_t)
    held = (h_one, h_other, across(h_one), merge(h_other, h_one))
    right_far, left_far, right_near, left_near, h_one, h_other, h_back, h_next = pack(where, tab, x, (0, 2, 1, 3), held)
    rf, lf = shift(right_far, 1), shift(left_far, -1)
    rn, ln = shift(right_near, 1), shift(left_near, -1)
    h_next = after(along(h_next), rf, lf, rn, ln)
    h_parts = [h_vals, h_other, h_one, h_back, h_next, across(h_next)]
    h_at = x[:, WIN * B : WIN * B + N_LAYER, 0 : K // N_LAYER].astype(jnp.int32)
    h_at = (h_at - own_row // GROUP * GROUP + 2 * GROUP) % NB
    h_at = h_at.reshape(2, N_LAYER, N_LAYER, K // N_LAYER).transpose(0, 2, 1, 3).reshape(GROUP, K)
    out_rows = jnp.arange(GROUP, dtype=jnp.int32)[:, None]
    is_near = jnp.logical_and(h_at >= GROUP, h_at < GROUP + NEAR)
    h_at = jnp.where(is_near, h_at - GROUP, NEAR + (h_at - out_rows) % GROUP)
    h_at = jnp.concatenate([h_at, absent(h_at, NEAR + GROUP)], axis=1)
    rff, lff = shift(rf, 1), shift(lf, -1)
    acc, far_h = near(where, tab, h_at, x, rf, rn, lf, ln, h_parts)
    sums = far(where, tab, acc, far_h, rff, lff)
    got = exchange(sums)
    return tuple(update(places, coefficient, got, density, t_prev))


def solution(mesh):
    rows = P(("grid", "layer"), None, None, None)
    placed = (P("grid", "layer", None, None), P("grid", "layer"), rows, rows, P(), rows, P())
    return jax.shard_map(shards, mesh=mesh, in_specs=placed, out_specs=(rows, rows), check_vma=False)
```

```python
import functools

import jax
import jax.numpy as jnp
import numpy as np
from jax import lax
from jax.experimental import pallas as pl
from jax.experimental.pallas import tpu as pltpu
from jax.sharding import PartitionSpec as P

HW = 15
B = 128
K = 28
NB = 256
N_LAYER = 4
GROUP = 8
WIN = 4
EXTRA = 16
ROWS = WIN * B + EXTRA
NEAR = 24
FAR = 7
WIDE = 5
MIB = 2**20


def halo_lists(step):
    far, near = [], []
    for cls in range(GROUP):
        got = {1: [], 2: []}
        for row in range(GROUP):
            for slot in range(WIN):
                col = cls + GROUP * (slot - 2 + (row > cls))
                if abs(col - row) > HW:
                    continue
                for dist in (1, 2):
                    at = GROUP * dist * step
                    if any(abs(out + at - row) <= HW and abs(out + at - col) <= HW for out in range(GROUP)):
                        got[dist].append(row * WIN + slot)
        assert set(got[2]) <= set(got[1])
        far.append(got[2])
        near.append([x for x in got[1] if x not in got[2]])
    return far, near


def table():
    lists = [*halo_lists(1), *halo_lists(-1)]
    sizes = [max(len(x) for x in part) for part in lists]
    rows = [sum(([*part[cls], *([-1] * (size - len(part[cls])))] for part, size in zip(lists, sizes)), []) for cls in range(GROUP)]
    return np.array(rows, np.int32), sizes


TABLE, SIZES = table()
STARTS = [sum(SIZES[:i]) for i in range(4)]


def whole(space=pltpu.VMEM):
    return pl.BlockSpec(memory_space=space)


def in_hbm(x):
    return pltpu.with_memory_space_constraint(x, pltpu.HBM)


def params(mib):
    return pltpu.CompilerParams(vmem_limit_bytes=mib * MIB)


def absent(present_at, size):
    every = jnp.arange(size, dtype=jnp.int32)
    missing = jnp.all(present_at[..., None, :] != every[:, None], axis=-1)
    rank = jnp.sum(jnp.where(every[None, :] < every[:, None], missing[..., None, :], False).astype(jnp.int32), axis=-1)
    wanted = jnp.arange(size - present_at.shape[-1], dtype=jnp.int32)
    hit = jnp.logical_and(missing[..., None, :], rank[..., None, :] == wanted[:, None])
    return jnp.sum(jnp.where(hit, every, 0), axis=-1)


def spread_kernel(where_ref, t_ref, cols_ref, h_cols_ref, out_ref, places_ref, cols, h_cols, tile, sems):
    row = where_ref[0]
    half = pl.multiple_of(row // B * B, B)
    load_cols = pltpu.make_async_copy(cols_ref.at[:, pl.ds(half, B)], cols, sems.at[0])
    load_h_cols = pltpu.make_async_copy(h_cols_ref, h_cols, sems.at[1])
    load_cols.start()
    load_h_cols.start()
    tile[...] = jnp.zeros_like(tile)
    for cls in range(GROUP):
        out_ref[cls, 0 : WIN * B, :] = jnp.zeros((WIN * B, B), jnp.bfloat16)
    load_cols.wait()
    for slot in range(K):
        ahead = (cols[slot, row % B] - row + NB // 2) % NB - NB // 2 + 2 * GROUP
        place = (row + ahead) % GROUP * WIN + ahead // GROUP
        places_ref[slot] = place
        start = pl.multiple_of(place % WIN * B, B)
        pltpu.make_async_copy(t_ref.at[0, slot], out_ref.at[place // WIN, pl.ds(start, B)], sems.at[2]).start()
    load_h_cols.wait()
    tile[0 : h_cols.shape[0], 0 : h_cols.shape[1]] = h_cols[...].astype(jnp.float32)
    for cls in range(GROUP):
        out_ref[cls, WIN * B : ROWS, :] = tile[...].astype(jnp.bfloat16)
    pltpu.make_async_copy(t_ref, t_ref, sems.at[2]).wait()


def spread(where, t_now, t_cols, h_cols):
    return pl.pallas_call(
        spread_kernel,
        out_shape=[jax.ShapeDtypeStruct((GROUP, ROWS, B), jnp.bfloat16), jax.ShapeDtypeStruct((K,), jnp.int32)],
        in_specs=[whole(pltpu.SMEM)] + [whole(pltpu.HBM)] * 3,
        out_specs=[whole(), whole(pltpu.SMEM)],
        scratch_shapes=[
            pltpu.SMEM((K, B), jnp.int32),
            pltpu.VMEM(h_cols.shape, jnp.int32),
            pltpu.VMEM((EXTRA, B), jnp.float32),
            pltpu.SemaphoreType.DMA((3,)),
        ],
        compiler_params=params(8),
        name="spread",
    )(where, *map(in_hbm, (t_now, t_cols.T, h_cols)))


def pack_kernel(where_ref, tab_ref, x_ref, _, *refs):
    *out_refs, sems = refs
    cls = where_ref[1]
    for number, (out_ref, first, size) in enumerate(zip(out_refs, STARTS, SIZES)):
        for at in range(size):
            entry = jnp.maximum(tab_ref[cls, first + at], 0)
            start = pl.multiple_of(entry % WIN * B, B)
            pltpu.make_async_copy(x_ref.at[entry // WIN, pl.ds(start, B)], out_ref.at[at], sems.at[number]).start()
    for number, out_ref in enumerate(out_refs):
        pltpu.make_async_copy(out_ref, out_ref, sems.at[number]).wait()


def pack(where, tab, x, before):
    return pl.pallas_call(
        pack_kernel,
        out_shape=[pltpu.HBM((size, B, B), jnp.bfloat16) for size in SIZES],
        in_specs=[whole(pltpu.SMEM), whole(pltpu.SMEM), whole(pl.ANY), whole(pl.ANY)],
        out_specs=[whole(pltpu.HBM)] * 4,
        scratch_shapes=[pltpu.SemaphoreType.DMA((4,))],
        compiler_params=params(4),
        name="pack",
    )(where, tab, x, before)


def merge_kernel(first_ref, second_ref, out_ref, sem):
    half = first_ref.shape[0]
    load = pltpu.make_async_copy(first_ref, out_ref.at[0:half], sem)
    load.start()
    out_ref[half:] = second_ref[...]
    load.wait()


def merge(first, second):
    return pl.pallas_call(
        merge_kernel,
        out_shape=jax.ShapeDtypeStruct((2 * first.shape[0], *first.shape[1:]), first.dtype),
        in_specs=[whole(pltpu.HBM), whole()],
        out_specs=whole(),
        scratch_shapes=[pltpu.SemaphoreType.DMA],
        compiler_params=params(8),
        name="merge",
    )(in_hbm(first), second)


def after_kernel(*_):
    pass


def after(*held, hide=0):
    return pl.pallas_call(
        after_kernel,
        out_shape=[jax.ShapeDtypeStruct(h.shape, h.dtype) for h in held],
        in_specs=[whole(pl.ANY)] * len(held),
        out_specs=[whole(pl.ANY)] * len(held),
        input_output_aliases={i: i for i in range(len(held))},
        compiler_params=params(4),
        cost_estimate=pl.CostEstimate(flops=hide, bytes_accessed=hide // 100, transcendentals=0),
        name="after",
    )(*held)


H_PARTS = (((0, 0),), ((0, 1),), ((-1, 0),), ((1, 1),), ((-1, 1), (2, 0)), ((1, 0), (2, 1)))


def near_kernel(where_ref, tab_ref, h_at_ref, x_ref, rf_ref, rn_ref, lf_ref, ln_ref, *refs):
    *h_refs, acc_ref, far_ref, hd, xd, sem = refs
    cls = where_ref[1]

    own_core = cls // N_LAYER
    for h_ref, parts in zip(h_refs, H_PARTS):
        for number, (apart, other) in enumerate(parts):
            core = 1 - own_core if other else own_core
            layer = (cls + apart * (1 - 2 * own_core) + N_LAYER) % N_LAYER

            @pl.loop(0, N_LAYER)
            def _(r):
                out_row = core * N_LAYER + r
                rows = pl.ds(pl.multiple_of(out_row * B, B), B)
                for slot in range(K // N_LAYER):
                    at = h_at_ref[out_row, layer * (K // N_LAYER) + slot]
                    if h_ref is h_refs[0] or h_ref is h_refs[1]:
                        pltpu.make_async_copy(h_ref.at[r, slot], hd.at[at, rows], sem).start()
                    else:
                        hd[at, rows, :] = h_ref[number * N_LAYER + r, slot]

    @pl.loop(0, GROUP)
    def _(out_row):
        rows = pl.ds(pl.multiple_of(out_row * B, B), B)
        for i in range(K, NEAR + GROUP):
            hd[h_at_ref[out_row, i], rows, :] = jnp.zeros((B, B), jnp.bfloat16)

    xd[...] = jnp.zeros_like(xd)
    for row in range(GROUP):
        for slot in range(WIN):
            xd[slot + (row > cls).astype(jnp.int32), (GROUP + row) * B : (GROUP + row + 1) * B, :] = x_ref[row, slot * B : (slot + 1) * B, :]
    for ref, first, size, dist in zip((rf_ref, rn_ref, lf_ref, ln_ref), STARTS, SIZES, (-1, -1, 1, 1)):
        for i in range(size):
            entry = tab_ref[cls, first + i]
            row, slot = entry // WIN, entry % WIN
            col = slot + (row > cls).astype(jnp.int32) + dist
            start = jnp.where(entry >= 0, (GROUP * (1 + dist) + row) * B, NEAR * B)
            xd[jnp.clip(col, 0, WIDE - 1), pl.ds(pl.multiple_of(start, B), B), :] = ref[i]

    pltpu.make_async_copy(hd.at[0 : K // N_LAYER], hd.at[0 : K // N_LAYER], sem).wait()

    @pl.loop(0, GROUP)
    def _(out_row):
        rows = pl.ds(pl.multiple_of(out_row * B, B), B)
        for i in range(GROUP):
            far_ref[i, rows, :] = hd[NEAR + i, rows, :]
        shift = (out_row > cls).astype(jnp.int32)
        left = jnp.concatenate([hd[n, rows, :] for n in range(NEAR)], axis=1)
        for slot in range(0, WIN, 2):
            right = jnp.concatenate([xd[slot + i + shift, 0 : NEAR * B, :] for i in range(2)], axis=1)
            got = jnp.dot(left, right, preferred_element_type=jnp.float32)
            for i in range(2):
                acc_ref[out_row, slot + i] = got[:, i * B : (i + 1) * B]


def near(where, tab, h_at, x, rf, rn, lf, ln, h_parts):
    return pl.pallas_call(
        near_kernel,
        out_shape=[
            jax.ShapeDtypeStruct((GROUP, WIN, B, B), jnp.float32),
            jax.ShapeDtypeStruct((GROUP, GROUP * B, B), jnp.bfloat16),
        ],
        in_specs=[whole(pltpu.SMEM)] * 3 + [whole()] * 5 + [whole(pltpu.HBM)] * 2 + [whole()] * (len(h_parts) - 2),
        out_specs=[whole()] * 2,
        scratch_shapes=[
            pltpu.VMEM((NEAR + GROUP, GROUP * B, B), jnp.bfloat16),
            pltpu.VMEM((WIDE, (NEAR + 1) * B, B), jnp.bfloat16),
            pltpu.SemaphoreType.DMA,
        ],
        compiler_params=params(22),
        cost_estimate=pl.CostEstimate(flops=2 * 1024 * 3072 * 512, bytes_accessed=20_000_000, transcendentals=0),
        name="near",
    )(where, tab, h_at, x, rf, rn, lf, ln, *map(in_hbm, h_parts[:2]), *h_parts[2:])


def far_kernel(where_ref, tab_ref, acc_ref, far_ref, r_ref, l_ref, out_ref, xd):
    cls = where_ref[1]
    xd[...] = jnp.zeros_like(xd)
    for ref, first, size, dist in ((r_ref, STARTS[0], SIZES[0], -2), (l_ref, STARTS[2], SIZES[2], 2)):
        for i in range(size):
            entry = tab_ref[cls, first + i]
            row, slot = entry // WIN, entry % WIN
            col = slot + (row > cls).astype(jnp.int32) + dist
            start = jnp.where(entry >= 0, (GROUP * (dist // 2 + 1) // 2 + row) * B, 2 * GROUP * B)
            xd[jnp.clip(col, 0, WIDE - 1), pl.ds(pl.multiple_of(start, B), B), :] = ref[i]

    @pl.loop(0, GROUP)
    def _(out_row):
        first = pl.multiple_of(out_row * B, B)
        shift = (out_row > cls).astype(jnp.int32)
        left = jnp.concatenate([far_ref[n, pl.ds(first, B), :] for n in range(GROUP)], axis=1)
        for slot in range(0, WIN, 2):
            right = jnp.concatenate([xd[slot + i + shift, pl.ds(first, GROUP * B), :] for i in range(2)], axis=1)
            got = jnp.dot(left, right, preferred_element_type=jnp.float32)
            for i in range(2):
                out_ref[out_row, slot + i] = (acc_ref[out_row, slot + i] + got[:, i * B : (i + 1) * B]).astype(jnp.bfloat16)


def far(where, tab, acc, far_h, fr, fl):
    return pl.pallas_call(
        far_kernel,
        out_shape=jax.ShapeDtypeStruct((GROUP, WIN, B, B), jnp.bfloat16),
        in_specs=[whole(pltpu.SMEM)] * 2 + [whole()] * 4,
        out_specs=whole(),
        scratch_shapes=[pltpu.VMEM((WIDE, (2 * GROUP + 1) * B, B), jnp.bfloat16)],
        compiler_params=params(16),
        cost_estimate=pl.CostEstimate(flops=2 * 1024 * 1024 * 512, bytes_accessed=8_000_000, transcendentals=0),
        name="far",
    )(where, tab, acc, far_h, fr, fl)


CHUNK = 4


def update_kernel(places_ref, coef_ref, got_ref, density_ref, prev_hbm, next_hbm, out_hbm, prev, fresh, out, prev_sem, next_sem, out_sem):
    def at(ref, part):
        return ref.at[0, part * CHUNK : (part + 1) * CHUNK]

    def copies(part):
        return (
            pltpu.make_async_copy(at(prev_hbm, part), at(prev, part), prev_sem.at[part]),
            pltpu.make_async_copy(at(fresh, part), at(next_hbm, part), next_sem.at[part]),
            pltpu.make_async_copy(at(out, part), at(out_hbm, part), out_sem.at[part]),
        )

    for part in range(K // CHUNK):
        copies(part)[0].start()
    for part in range(K // CHUNK):
        load, *stores = copies(part)
        load.wait()
        for slot in range(part * CHUNK, (part + 1) * CHUNK):
            place = places_ref[slot]
            product = got_ref[place // WIN, place % WIN].astype(jnp.float32)
            value = (2.0 * product - prev[0, slot].astype(jnp.float32)).astype(jnp.bfloat16)
            fresh[0, slot] = value
            out[0, slot] = density_ref[0, slot] + coef_ref[0] * value.astype(jnp.float32)
        for store in stores:
            store.start()
    for part in range(K // CHUNK):
        copies(part)[1].wait()
        copies(part)[2].wait()


def update(places, coefficient, got, density, t_prev):
    shape = (1, K, B, B)
    sems = pltpu.SemaphoreType.DMA((K // CHUNK,))
    return pl.pallas_call(
        update_kernel,
        out_shape=[jax.ShapeDtypeStruct(shape, jnp.bfloat16), jax.ShapeDtypeStruct(shape, jnp.float32)],
        in_specs=[whole(pltpu.SMEM), whole(pltpu.SMEM), whole(), whole(), whole(pltpu.HBM)],
        out_specs=[whole(pltpu.HBM)] * 2,
        scratch_shapes=[pltpu.VMEM(shape, jnp.bfloat16), pltpu.VMEM(shape, jnp.bfloat16), pltpu.VMEM(shape, jnp.float32), sems, sems, sems],
        compiler_params=params(16),
        name="update",
    )(places, coefficient, got, density, in_hbm(t_prev))


def shards(h_vals, h_cols, t_now, t_prev, t_cols, density, coefficient):
    chips = lax.axis_size("grid") // 2
    groups = [[(2 * q + core) * N_LAYER + x for core in range(2) for x in range(N_LAYER)] for q in range(chips)]
    axes = ("grid", "layer")
    exchange = functools.partial(lax.all_to_all, axis_name=axes, split_axis=0, concat_axis=0, axis_index_groups=groups, tiled=True)

    def shift(block, step):
        count = lax.axis_size("grid")
        return lax.ppermute(block, "grid", [(i, (i + 2 * step) % count) for i in range(count)])

    def along(block):
        route = [(g * N_LAYER + x, g * N_LAYER + (x + 1 - 2 * (g % 2)) % N_LAYER) for g in range(2 * chips) for x in range(N_LAYER)]
        return lax.ppermute(block, axes, route)

    def across(block):
        return lax.ppermute(block, "grid", [(i, i ^ 1) for i in range(2 * chips)])

    own_row = lax.axis_index("grid") * N_LAYER + lax.axis_index("layer")
    where = jnp.stack([own_row, own_row % GROUP]).astype(jnp.int32)
    tab = jnp.asarray(TABLE)

    h_one, h_other = along(h_vals), across(h_vals)
    spread_t, places = spread(where, t_now, t_cols, h_cols)
    x = exchange(spread_t)
    h_back = across(h_one)
    right_far, right_near, left_far, left_near = pack(where, tab, x, h_back)
    rf, lf = shift(right_far, 1), shift(left_far, -1)
    rn, ln = shift(right_near, 1), shift(left_near, -1)
    h_next = along(merge(h_other, h_one))
    (h_last,) = after(across(h_next), hide=10**12)
    h_parts = [h_vals, h_other, h_one, h_back, h_next, h_last]
    h_at = x[:, WIN * B : WIN * B + N_LAYER, 0 : K // N_LAYER].astype(jnp.int32)
    h_at = (h_at - own_row // GROUP * GROUP + 2 * GROUP) % NB
    h_at = h_at.reshape(2, N_LAYER, N_LAYER, K // N_LAYER).transpose(0, 2, 1, 3).reshape(GROUP, K)
    out_rows = jnp.arange(GROUP, dtype=jnp.int32)[:, None]
    is_near = jnp.logical_and(h_at >= GROUP, h_at < GROUP + NEAR)
    h_at = jnp.where(is_near, h_at - GROUP, NEAR + (h_at - out_rows) % GROUP)
    h_at = jnp.concatenate([h_at, absent(h_at, NEAR + GROUP)], axis=1)
    rf, lf = after(rf, lf, hide=10**12)
    rff, lff = shift(rf, 1), shift(lf, -1)
    acc, far_h = near(where, tab, h_at, x, rf, rn, lf, ln, h_parts)
    sums = far(where, tab, acc, far_h, rff, lff)
    got = exchange(sums)
    return tuple(update(places, coefficient, got, density, t_prev))


def solution(mesh):
    rows = P(("grid", "layer"), None, None, None)
    placed = (P("grid", "layer", None, None), P("grid", "layer"), rows, rows, P(), rows, P())
    return jax.shard_map(shards, mesh=mesh, in_specs=placed, out_specs=(rows, rows), check_vma=False)
```
